32 devices in a mesh: rows: 32 (over z, y, x, core), rep: 1.
Axes of the slice: x: 2, y: 2, z: 4, core: 2. Of those that a mesh axis runs over, the one named last changes fastest.
Arguments:
- features: bfloat16 [32768, 128], P(('rows', 'rep')), may hold values from -6 to 6
- weight: bfloat16 [128, 256], replicated, may hold values from -0.5 to 0.5
- shift_bias: float32 [256], replicated, may hold values from -3 to 3
- norm_gain: float32 [256], replicated, may hold values from 0.25 to 1.75
- tile_values: bfloat16 [256, 1, 88, 128, 128], P('rows', 'rep'), as said below
- tile_cols: int32 [256, 1, 88], P('rows', 'rep'), may hold values from 0 to 255, all different within a row
- tile_counts: int32 [256, 1], P('rows', 'rep'), may hold values from 1 to 88, as said below
- block_order: int32 [1, 256], replicated, may hold values from 0 to 255, each once within a row
Outputs:
- node_out: bfloat16 [32768, 256], P(('rows', 'rep'))
The draws below stay inside these ranges and needn't reach their ends.
Inputs may be any that keep to these rules, and one draw needn't show every extreme that they name: Slots 0 to tile_counts - 1 of a row block and column set are live, the rest are ignored; the largest count is reached. `tile_values`: tile entries are nonnegative.
All inputs are finite; a program needn't handle non-finite values.
Results may differ from the reference program's by a relative error of at most 0.0052.
Values may be sent and summed in bfloat16 or wider, within the bound.
A program may use at most 192 MiB of HBM per device.

```python
import math
import jax
import jax.numpy as jnp
from jax import lax

F = 128
H = 256
BLK = 128
RB_DEV = 8
NBLK = 256
NSET = 256
KR = 88
NODES = 32768
N_ROWS = 32
N_REP = 1


def draw_tile_values(key, part):
    shape = (NBLK, N_REP, KR, BLK, BLK)
    scale = 1.0 / math.sqrt(BLK * KR // 2)
    values = jnp.abs(jax.random.normal(key, shape, jnp.float32)) * scale
    return values.astype(jnp.bfloat16)


def draw_tile_counts(key, part):
    key_heavy, key_high, key_low, key_spot = jax.random.split(key, 4)
    heavy = jax.random.randint(key_heavy, (NBLK, N_REP), 0, 4) == 0
    high_counts = jax.random.randint(key_high, (NBLK, N_REP), KR // 2, KR + 1)
    low_counts = jax.random.randint(key_low, (NBLK, N_REP), 1, KR // 2 + 1)
    values = jnp.where(heavy, high_counts, low_counts).reshape(-1)
    spot = jax.random.randint(key_spot, (), 0, NBLK * N_REP)
    values = jnp.where(jnp.arange(NBLK * N_REP) == spot, KR, values)
    return values.reshape(NBLK, N_REP).astype(jnp.int32)


def levels(rng, shape, cuts, least, top_value):
    factor_of, own = 1.0, jax.random.fold_in(rng, 6)
    for dim, shards_of in cuts:
        heights = jnp.exp(jax.random.uniform(jax.random.fold_in(own, dim), (shards_of,), jnp.float32, least / len(cuts), top_value / len(cuts)))
        factor_of = factor_of * jnp.repeat(heights, shape[dim] // shards_of).reshape([-1 if axis == dim else 1 for axis in range(len(shape))])
    return factor_of


def choose_distinct(rng, rows, number_of, top, lift):
    ranking = jax.random.permutation(jax.random.fold_in(rng, 1), number_of)
    favour = ranking
    for power in range(3):
        favour = favour * favour // number_of
    favour = favour * lift // number_of
    chance = jax.random.randint(jax.random.fold_in(rng, 2), (rows, number_of), 0, 4096) + favour
    fixed_rows = jax.random.permutation(jax.random.fold_in(rng, 3), rows)[jnp.arange(number_of) % rows]
    chance = jnp.where(jnp.arange(rows)[:, None] == fixed_rows[None, :], 1 << 14, chance)
    priority = chance * number_of + jnp.arange(number_of)
    return lax.top_k(priority.astype(jnp.int32), top)[1].astype(jnp.int32)


def normal_values(rng, shape, spread, bound, cuts=(), dtype=jnp.bfloat16):
    drawn = jax.random.normal(rng, shape, jnp.float32) * spread
    if len(cuts) > 0:
        drawn = levels(rng, shape, cuts, -0.22, 0.18) * drawn
    return jnp.clip(drawn, min=-bound, max=bound).astype(dtype)


def setup_inputs(seed: int = 0) -> dict:
    splits = jax.random.split(jax.random.key(seed), 9)
    return {
        "features": normal_values(splits[0], (NODES, F), 1.0, 6.0, ((0, 32),)),
        "weight": normal_values(splits[1], (F, H), F ** -0.5, 0.5),
        "shift_bias": normal_values(splits[2], (H,), 0.5, 3.0, (), jnp.float32),
        "norm_gain": jnp.clip(1.0 + 0.15 * jax.random.normal(splits[3], (H,), jnp.float32), 0.25, 1.75),
        "tile_values": draw_tile_values(jax.random.fold_in(splits[8], 71), 0),
        "tile_cols": choose_distinct(splits[5], NBLK * N_REP, NSET, KR, 0).reshape((NBLK, N_REP, KR)),
        "tile_counts": draw_tile_counts(jax.random.fold_in(splits[8], 71), 0),
        "block_order": jax.vmap(lambda own: jax.random.permutation(own, NSET))(jax.random.split(splits[7], N_REP)).reshape((N_REP, NSET)).astype(jnp.int32),
    }


def reference(features, weight, shift_bias, norm_gain, tile_values, tile_cols, tile_counts, block_order):
    projected = jnp.dot(features, weight, preferred_element_type=jnp.float32).astype(jnp.bfloat16)
    half_owner = RB_DEV // N_REP
    column_sets = projected.reshape(N_ROWS, N_REP, half_owner, BLK, H)
    column_sets = jnp.transpose(column_sets, (1, 0, 2, 3, 4)).reshape(N_REP, NSET, BLK, H)

    def one_block(inputs):
        block_tiles, block_cols, block_counts = inputs
        running = jnp.zeros((BLK, H), jnp.float32)
        for replica in range(N_REP):
            positions = block_order[replica][block_cols[replica]]
            picked_rows = column_sets[replica][positions].astype(jnp.float32)
            live_mask = jnp.arange(KR) < block_counts[replica]
            picked_rows = jnp.where(live_mask[:, None, None], picked_rows, jnp.float32(0.0))
            running = running + jnp.einsum('kij,kjh->ih', block_tiles[replica].astype(jnp.float32), picked_rows)
        return running
    summed = lax.map(one_block, (tile_values, tile_cols, tile_counts))
    hidden = jnp.maximum(summed.reshape(NODES, H) + shift_bias, 0.0)
    row_mean = lax.optimization_barrier(jnp.mean(hidden, axis=1, keepdims=True))
    centered = hidden - row_mean
    row_var = lax.optimization_barrier(jnp.mean(centered * centered, axis=1, keepdims=True))
    return (centered / jnp.sqrt(row_var + 1e-05) * norm_gain).astype(jnp.bfloat16)
```

```python
import functools

import jax
import jax.numpy as jnp
from jax import lax
from jax.experimental import pallas as pl
from jax.experimental.pallas import tpu as pltpu
from jax.sharding import PartitionSpec as P

MESH = pl.DeviceIdType.MESH

ORDERS = ("xzy", "yzx", "zxy", "zyx")


def normed(hidden, gain):
    row_mean = jnp.mean(hidden, axis=1, keepdims=True)
    centered = hidden - row_mean
    row_var = jnp.mean(centered * centered, axis=1, keepdims=True)
    return (centered / jnp.sqrt(row_var + 1e-05) * gain).astype(jnp.bfloat16)


def kernel(
    rows, fuse_norm, feat, weight, bias, gain, lookup, tiles, out,
    panel, held, acc, send_sem, recv_sem, own_sem, tile_sem,
):
    depth_z = rows // 8
    steps = depth_z * 4
    shard_rows = feat.shape[0]
    piece_rows = shard_rows // len(ORDERS)
    row_blocks, slots, block = tiles.shape[0], tiles.shape[1], tiles.shape[2]
    shard_blocks = shard_rows // block

    me = lax.axis_index("rows")
    core = me % 2
    x = (me // 2) % 2
    y = (me // 4) % 2
    z = me // 8
    x_peer = me + 2 - 4 * x
    y_peer = me + 4 - 8 * y
    core_peer = me + 1 - 2 * core
    up, down = me + 8, me - 8
    has_up, has_down = z < depth_z - 1, z > 0

    own = pltpu.make_async_copy(feat, panel.at[me], own_sem)
    own.start()

    barrier = pltpu.get_barrier_semaphore()
    for peer in (x_peer, y_peer, core_peer):
        pl.semaphore_signal(barrier, inc=1, device_id={"rows": peer}, device_id_type=MESH)

    @pl.when(has_up)
    def _():
        pl.semaphore_signal(barrier, inc=1, device_id={"rows": up}, device_id_type=MESH)

    @pl.when(has_down)
    def _():
        pl.semaphore_signal(barrier, inc=1, device_id={"rows": down}, device_id_type=MESH)

    pl.semaphore_wait(barrier, 3 + jnp.where(has_up, 1, 0) + jnp.where(has_down, 1, 0))

    def source(s):
        j, ey, ex = s // 4, (s // 2) % 2, s % 2
        low = z < depth_z - 1 - z
        near = jnp.where(low, z, depth_z - 1 - z)
        far_way = jnp.where(low, 1, -1)
        both = j <= 2 * near
        distance = jnp.where(both, (j + 1) // 2, j - near)
        way = jnp.where(jnp.logical_and(both, j % 2 == 1), -far_way, far_way)
        zs = z + way * distance
        ys, xs = (y + ey) % 2, (x + ex) % 2
        chip = (zs * 2 + ys) * 2 + xs
        return chip, zs, ey, ex

    def piece(cls, origin):
        return panel.at[origin, pl.ds(cls * piece_rows, piece_rows)]

    def copy(cls, origin, way, s, peer):
        return pltpu.make_async_remote_copy(
            src_ref=piece(cls, origin),
            dst_ref=piece(cls, origin),
            send_sem=send_sem.at[cls, way, s],
            recv_sem=recv_sem.at[cls, origin],
            device_id={"rows": peer},
            device_id_type=MESH,
        )

    def sends(cls, s, act):
        chip, zs, ey, ex = source(s)
        origin = chip * 2 + core
        still = {"x": ex == 0, "y": ey == 0, "z": zs == z}
        order = ORDERS[cls]

        def clear(axis):
            later = [still[a] for a in order[order.index(axis) + 1:]]
            return functools.reduce(jnp.logical_and, later, s >= 0)

        plan = (
            (0, up, clear("z") & has_up & (zs <= z)),
            (1, down, clear("z") & has_down & (zs >= z)),
            (2, x_peer, clear("x") & still["x"]),
            (3, y_peer, clear("y") & still["y"]),
        )
        for way, peer, cond in plan:
            pl.when(cond)(functools.partial(act, cls, origin, way, s, peer))
        act(cls, origin, 4, s, core_peer)

    def start(*what):
        copy(*what).start()

    def finish(*what):
        copy(*what).wait_send()

    acc[...] = jnp.zeros_like(acc)
    for b in range(row_blocks):
        held[b, slots] = jnp.zeros(held.shape[2:], held.dtype)
    own.wait()

    tile_copies = [
        pltpu.make_async_copy(tiles.at[b], held.at[b, pl.ds(0, slots)], tile_sem.at[b])
        for b in range(row_blocks)
    ]

    def multiply(q, carry):
        chip = source(q // 2)[0]
        origin = chip * 2 + (core + q) % 2

        @pl.when(q % 2 == 1)
        def _():
            for cls in range(len(ORDERS)):
                copy(cls, origin, 4, 0, core_peer).wait_recv()

        first = origin * shard_blocks
        left = jnp.concatenate(
            [
                jnp.concatenate(
                    [held[b, lookup[b, first + c]] for c in range(shard_blocks)], axis=1
                )
                for b in range(row_blocks)
            ],
            axis=0,
        )
        acc[...] += jnp.dot(left, panel[origin], preferred_element_type=jnp.float32)
        return carry

    def done_after(s):
        return jnp.maximum(0, jnp.minimum(2 * s + 1, 4 * s - 8))

    def step(s, carry):
        @pl.when(s < steps)
        def _():
            origin = source(s)[0] * 2 + core
            for cls in range(len(ORDERS)):
                @pl.when(s > 0)
                def _():
                    copy(cls, origin, 4, 0, core_peer).wait_recv()

                sends(cls, s, start)

        @pl.when(s == 0)
        def _():
            for c in tile_copies:
                c.start()

        @pl.when(s == 3)
        def _():
            for c in tile_copies:
                c.wait()

        lax.fori_loop(done_after(s - 1), jnp.minimum(done_after(s), 2 * steps), multiply, 0)
        return carry

    lax.fori_loop(0, steps + 1, step, 0)

    w = weight[...]
    for b in range(row_blocks):
        part = pl.ds(b * block, block)
        total = acc[part]
        high = total.astype(jnp.bfloat16)
        rest = (total - high.astype(jnp.float32)).astype(jnp.bfloat16)
        summed = jnp.dot(high, w, preferred_element_type=jnp.float32)
        summed += jnp.dot(rest, w, preferred_element_type=jnp.float32)
        if fuse_norm:
            out[part] = normed(jnp.maximum(summed + bias[...], 0.0), gain[...])
        else:
            out[part] = summed

    def drain(s, carry):
        for cls in range(len(ORDERS)):
            sends(cls, s, finish)
        return carry

    lax.fori_loop(0, steps, drain, 0)


def per_device(
    rows, reps, features, weight, shift_bias, norm_gain, tile_values, tile_cols, tile_counts, block_order
):
    row_blocks, _, slots, block, _ = tile_values.shape
    shard_rows, width = features.shape
    hidden_width = weight.shape[1]
    set_blocks = rows * shard_rows // block
    order = lax.dynamic_index_in_dim(block_order, lax.axis_index("rep"), 0, keepdims=False)
    numbers = jnp.arange(set_blocks, dtype=jnp.int32)
    number_at = jnp.sum(jnp.where(order[:, None] == numbers[None, :], numbers[:, None], 0), axis=0)
    ids = tile_cols.reshape(row_blocks, slots)
    slot = jnp.arange(slots, dtype=jnp.int32)[None, :]
    ids = jnp.where(slot < tile_counts.reshape(row_blocks, 1), ids, -1)
    hit = ids[:, :, None] == number_at[None, None, :]
    lookup = slots + jnp.sum(jnp.where(hit, slot[:, :, None] - slots, 0), axis=1)

    fuse_norm = reps == 1
    nodes = row_blocks * block
    vmem = pl.BlockSpec(memory_space=pltpu.VMEM)
    hbm = pl.BlockSpec(memory_space=pl.ANY)
    summed = pl.pallas_call(
        functools.partial(kernel, rows, fuse_norm),
        out_shape=jax.ShapeDtypeStruct(
            (nodes, hidden_width), jnp.bfloat16 if fuse_norm else jnp.float32
        ),
        in_specs=[hbm, vmem, vmem, vmem, pl.BlockSpec(memory_space=pltpu.SMEM), hbm],
        out_specs=vmem,
        scratch_shapes=[
            pltpu.VMEM((rows, shard_rows, width), jnp.bfloat16),
            pltpu.VMEM((row_blocks, slots + 1, block, block), jnp.bfloat16),
            pltpu.VMEM((nodes, width), jnp.float32),
            pltpu.SemaphoreType.DMA((len(ORDERS), 5, rows // 2)),
            pltpu.SemaphoreType.DMA((len(ORDERS), rows)),
            pltpu.SemaphoreType.DMA,
            pltpu.SemaphoreType.DMA((row_blocks,)),
        ],
        compiler_params=pltpu.CompilerParams(
            collective_id=0, has_side_effects=True, vmem_limit_bytes=52 * 1024 * 1024
        ),
    )(
        features, weight, shift_bias[None, :], norm_gain[None, :], lookup,
        tile_values.reshape(row_blocks, slots, block, block),
    )
    if fuse_norm:
        return summed
    mine = lax.psum_scatter(summed, "rep", scatter_dimension=0, tiled=True)
    return normed(jnp.maximum(mine + shift_bias, 0.0), norm_gain)


def solution(mesh):
    in_specs = (
        P(("rows", "rep"), None),
        P(),
        P(),
        P(),
        P("rows", "rep", None, None, None),
        P("rows", "rep", None),
        P("rows", "rep"),
        P(),
    )
    out_specs = P(("rows", "rep"), None)
    return jax.shard_map(
        functools.partial(per_device, mesh.shape["rows"], mesh.shape["rep"]),
        mesh=mesh, in_specs=in_specs, out_specs=out_specs, check_vma=False,
    )
```

```python
import functools
import heapq

import jax
import jax.numpy as jnp
from jax import lax
from jax.experimental import pallas as pl
from jax.experimental.pallas import tpu as pltpu
from jax.sharding import PartitionSpec as P

MESH = pl.DeviceIdType.MESH

ORDERS = ("xzy", "yzx", "zxy", "zyx")


def normed(hidden, gain):
    row_mean = jnp.mean(hidden, axis=1, keepdims=True)
    centered = hidden - row_mean
    row_var = jnp.mean(centered * centered, axis=1, keepdims=True)
    return (centered / jnp.sqrt(row_var + 1e-05) * gain).astype(jnp.bfloat16)


def visit(depth, z, s, choose):
    j = s // 4
    low = z < depth - 1 - z
    near = choose(low, z, depth - 1 - z)
    far_way = choose(low, 1, -1)
    both = j <= 2 * near
    distance = choose(both, (j + 1) // 2, j - near)
    way = choose(both & (j % 2 == 1), -far_way, far_way)
    return z + way * distance


def arrivals(depth, program):
    chips = [(z, y, x) for z in range(depth) for y in range(2) for x in range(2)]
    events = [(0.0, k, chip, None) for k, chip in enumerate(chips)]
    count, free, seen, at = len(events), {}, {}, dict.fromkeys(chips, 0)

    def forward(chip, cls, origin, now):
        nonlocal count
        order = ORDERS[cls]
        for axis, step in (("z", 1), ("z", -1), ("y", 0), ("x", 0)):
            k = "zyx".index(axis)
            if any(chip["zyx".index(a)] != origin["zyx".index(a)] for a in order[order.index(axis) + 1:]):
                continue
            if axis == "z":
                target = chip[0] + step
                if not 0 <= target < depth or (chip[0] - origin[0]) * step < 0:
                    continue
            elif chip[k] != origin[k]:
                continue
            else:
                target = 1 - chip[k]
            peer = chip[:k] + (target,) + chip[k + 1:]
            end = max(free.get((chip, peer), 0.0), now) + 1.0
            free[chip, peer] = end
            heapq.heappush(events, (end + 0.55, count, peer, (cls, origin)))
            count += 1

    while events:
        now, _, chip, item = heapq.heappop(events)
        if item is not None:
            seen[(chip,) + item] = now
        if program is None:
            for cls, origin in [item] if item else [(c, chip) for c in range(len(ORDERS))]:
                forward(chip, cls, origin, now)
            continue
        while at[chip] < len(program):
            cls, s = program[at[chip]]
            z, y, x = chip
            origin = (visit(depth, z, s, lambda c, a, b: a if c else b), (y + s // 2) % 2, (x + s) % 2)
            if s > 0 and (chip, cls, origin) not in seen:
                break
            forward(chip, cls, origin, now)
            at[chip] += 1
    return chips, seen


def make_program(depth):
    program = None
    for _ in range(2):
        chips, seen = arrivals(depth, program)
        total = {}
        for z, y, x in chips:
            for cls in range(len(ORDERS)):
                for s in range(1, 4 * depth):
                    origin = (visit(depth, z, s, lambda c, a, b: a if c else b), (y + s // 2) % 2, (x + s) % 2)
                    total[cls, s] = total.get((cls, s), 0.0) + seen[(z, y, x), cls, origin]
        program = [(cls, 0) for cls in range(len(ORDERS))]
        program += sorted(total, key=lambda item: (round(total[item], 6), item))
    return program


def kernel(
    rows, program, fuse_norm, feat, weight_hbm, bias_hbm, gain_hbm, lookup_hbm, tiles, out,
    panel, held, acc, weight, bias, gain, lookup, send_sem, recv_sem, own_sem, tile_sem, small_sem,
):
    depth_z = rows // 8
    steps = depth_z * 4
    items = len(program)
    shard_rows, width = feat.shape
    piece_rows = shard_rows // len(ORDERS)
    row_blocks, slots, block = tiles.shape[0], tiles.shape[1], tiles.shape[2]
    shard_blocks = shard_rows // block
    piece_blocks = piece_rows // block

    me = lax.axis_index("rows")
    core = me % 2
    x = (me // 2) % 2
    y = (me // 4) % 2
    z = me // 8
    x_peer = me + 2 - 4 * x
    y_peer = me + 4 - 8 * y
    core_peer = me + 1 - 2 * core
    up, down = me + 8, me - 8
    has_up, has_down = z < depth_z - 1, z > 0

    own = pltpu.make_async_copy(feat, panel.at[me], own_sem)
    own.start()

    barrier = pltpu.get_barrier_semaphore()
    for peer in (x_peer, y_peer, core_peer):
        pl.semaphore_signal(barrier, inc=1, device_id={"rows": peer}, device_id_type=MESH)

    @pl.when(has_up)
    def _():
        pl.semaphore_signal(barrier, inc=1, device_id={"rows": up}, device_id_type=MESH)

    @pl.when(has_down)
    def _():
        pl.semaphore_signal(barrier, inc=1, device_id={"rows": down}, device_id_type=MESH)

    small_copies = [
        pltpu.make_async_copy(there, here, small_sem.at[k])
        for k, (there, here) in enumerate(
            ((lookup_hbm, lookup), (weight_hbm, weight), (bias_hbm, bias), (gain_hbm, gain))
        )
    ]
    tile_copies = [
        pltpu.make_async_copy(tiles.at[b], held.at[b, pl.ds(0, slots)], tile_sem.at[b])
        for b in range(row_blocks)
    ]
    for c in small_copies + tile_copies:
        c.start()
    own.wait()
    pl.semaphore_wait(barrier, 3 + jnp.where(has_up, 1, 0) + jnp.where(has_down, 1, 0))

    def chip_of(s):
        zs = visit(depth_z, z, s, jnp.where)
        return (zs * 2 + (y + s // 2) % 2) * 2 + (x + s) % 2, zs

    def copy(cls, origin, sem, peer):
        piece = panel.at[origin, pl.ds(cls * piece_rows, piece_rows)]
        return pltpu.make_async_remote_copy(
            src_ref=piece,
            dst_ref=piece,
            send_sem=send_sem.at[sem],
            recv_sem=recv_sem.at[cls, origin],
            device_id={"rows": peer},
            device_id_type=MESH,
        )

    numbers = {}

    def take(cls, s, act):
        chip, zs = chip_of(s)
        origin = chip * 2 + core
        order = ORDERS[cls]
        still = {"x": s % 2 == 0, "y": (s // 2) % 2 == 0, "z": s < 4}

        def send(name, peer, cond=None):
            sem = numbers.setdefault((cls, s, name), len(numbers))
            if cond is None:
                act(cls, origin, sem, peer)
            else:
                pl.when(cond)(functools.partial(act, cls, origin, sem, peer))

        def clear(axis):
            return all(still[a] for a in order[order.index(axis) + 1:])

        if clear("z"):
            if still["z"]:
                send("up", up, has_up)
                send("down", down, has_down)
            else:
                send("up", up, has_up & (zs < z))
                send("down", down, has_down & (zs > z))
        if clear("y") and still["y"]:
            send("y", y_peer)
        if clear("x") and still["x"]:
            send("x", x_peer)
        send("core", core_peer)

    def start(*what):
        copy(*what).start()

    def finish(*what):
        copy(*what).wait_send()

    def item_step(k):
        cls, s = program[k]
        if s > 0:
            copy(cls, chip_of(s)[0] * 2 + core, 0, core_peer).wait_recv()
        take(cls, s, start)

    def dispatch(i, low, high):
        if high - low == 1:
            item_step(low)
            return
        middle = (low + high) // 2
        pl.when(i < middle)(lambda: dispatch(i, low, middle))
        pl.when(i >= middle)(lambda: dispatch(i, middle, high))

    bits = (items - 1).bit_length()
    per_word = 30 // bits
    words = [
        sum((cls * steps + s) << (bits * k) for k, (cls, s) in enumerate(program[w:w + per_word]))
        for w in range(0, items, per_word)
    ]

    def entry(q):
        which = q // per_word
        word = jnp.int32(words[0])
        for k in range(1, len(words)):
            word = jnp.where(which == k, words[k], word)
        code = lax.shift_right_logical(word, (q - which * per_word) * bits) & (2**bits - 1)
        return code // steps, code % steps

    def multiply(q, carry):
        cls, s = entry(q)
        chip = chip_of(s)[0]
        copy(cls, chip * 2 + 1 - core, 0, core_peer).wait_recv()
        right = panel[pl.ds(chip * 2, 2), pl.ds(pl.multiple_of(cls * piece_rows, piece_rows), piece_rows)]
        right = right.reshape(2 * piece_rows, width)
        columns = [
            (chip * 2 + c) * shard_blocks + cls * piece_blocks + k
            for c in range(2) for k in range(piece_blocks)
        ]
        left = jnp.concatenate(
            [
                jnp.concatenate([held[b, lookup[b, c]] for c in columns], axis=1)
                for b in range(row_blocks)
            ],
            axis=0,
        )
        acc[...] += jnp.dot(left, right, preferred_element_type=jnp.float32)
        return carry

    acc[...] = jnp.zeros_like(acc)
    for b in range(row_blocks):
        held[b, slots] = jnp.zeros(held.shape[2:], held.dtype)

    begin = items * 3 // 16

    def done_after(i):
        return jnp.maximum(0, jnp.minimum(i, (i - begin) * 3 // 2))

    def step(i, carry):
        pl.when(i < items)(lambda: dispatch(i, 0, items))

        @pl.when(i == begin)
        def _():
            for c in small_copies + tile_copies:
                c.wait()

        lax.fori_loop(done_after(i - 1), done_after(i), multiply, 0)
        return carry

    lax.fori_loop(0, items + 1, step, 0)

    w = weight[...]
    for b in range(row_blocks):
        part = pl.ds(b * block, block)
        total = acc[part]
        high = total.astype(jnp.bfloat16)
        rest = (total - high.astype(jnp.float32)).astype(jnp.bfloat16)
        summed = jnp.dot(high, w, preferred_element_type=jnp.float32)
        summed += jnp.dot(rest, w, preferred_element_type=jnp.float32)
        if fuse_norm:
            out[part] = normed(jnp.maximum(summed + bias[...], 0.0), gain[...])
        else:
            out[part] = summed

    for cls, s in program:
        take(cls, s, finish)


def per_device(
    rows, reps, program, features, weight, shift_bias, norm_gain, tile_values, tile_cols, tile_counts, block_order
):
    row_blocks, _, slots, block, _ = tile_values.shape
    shard_rows, width = features.shape
    hidden_width = weight.shape[1]
    set_blocks = rows * shard_rows // block
    order = lax.dynamic_index_in_dim(block_order, lax.axis_index("rep"), 0, keepdims=False)
    numbers = jnp.arange(set_blocks, dtype=jnp.int32)
    number_at = jnp.sum(jnp.where(order[:, None] == numbers[None, :], numbers[:, None], 0), axis=0)
    ids = tile_cols.reshape(row_blocks, slots)
    slot = jnp.arange(slots, dtype=jnp.int32)[None, :]
    ids = jnp.where(slot < tile_counts.reshape(row_blocks, 1), ids, -1)
    hit = ids[:, :, None] == number_at[None, None, :]
    lookup = slots + jnp.sum(jnp.where(hit, slot[:, :, None] - slots, 0), axis=1)

    fuse_norm = reps == 1
    nodes = row_blocks * block
    vmem = pl.BlockSpec(memory_space=pltpu.VMEM)
    hbm = pl.BlockSpec(memory_space=pl.ANY)
    summed = pl.pallas_call(
        functools.partial(kernel, rows, program, fuse_norm),
        out_shape=jax.ShapeDtypeStruct(
            (nodes, hidden_width), jnp.bfloat16 if fuse_norm else jnp.float32
        ),
        in_specs=[hbm] * 6,
        out_specs=vmem,
        scratch_shapes=[
            pltpu.VMEM((rows, shard_rows, width), jnp.bfloat16),
            pltpu.VMEM((row_blocks, slots + 1, block, block), jnp.bfloat16),
            pltpu.VMEM((nodes, width), jnp.float32),
            pltpu.VMEM(weight.shape, weight.dtype),
            pltpu.VMEM((1, hidden_width), jnp.float32),
            pltpu.VMEM((1, hidden_width), jnp.float32),
            pltpu.SMEM(lookup.shape, jnp.int32),
            pltpu.SemaphoreType.DMA((5 * len(program),)),
            pltpu.SemaphoreType.DMA((len(ORDERS), rows)),
            pltpu.SemaphoreType.DMA,
            pltpu.SemaphoreType.DMA((row_blocks,)),
            pltpu.SemaphoreType.DMA((4,)),
        ],
        compiler_params=pltpu.CompilerParams(
            collective_id=0, has_side_effects=True, vmem_limit_bytes=52 * 1024 * 1024
        ),
    )(
        features, weight, shift_bias[None, :], norm_gain[None, :], lookup,
        tile_values.reshape(row_blocks, slots, block, block),
    )
    if fuse_norm:
        return summed
    mine = lax.psum_scatter(summed, "rep", scatter_dimension=0, tiled=True)
    return normed(jnp.maximum(mine + shift_bias, 0.0), norm_gain)


def solution(mesh):
    program = make_program(mesh.shape["rows"] // 8)
    in_specs = (
        P(("rows", "rep"), None),
        P(),
        P(),
        P(),
        P("rows", "rep", None, None, None),
        P("rows", "rep", None),
        P("rows", "rep"),
        P(),
    )
    out_specs = P(("rows", "rep"), None)
    return jax.shard_map(
        functools.partial(per_device, mesh.shape["rows"], mesh.shape["rep"], program),
        mesh=mesh, in_specs=in_specs, out_specs=out_specs, check_vma=False,
    )
```

```python
import functools
import heapq

import jax
import jax.numpy as jnp
from jax import lax
from jax.experimental import pallas as pl
from jax.experimental.pallas import tpu as pltpu
from jax.sharding import PartitionSpec as P

MESH = pl.DeviceIdType.MESH

ORDERS = ("xzy", "yzx", "zxy", "zyx")


def normed(hidden, gain):
    row_mean = jnp.mean(hidden, axis=1, keepdims=True)
    centered = hidden - row_mean
    row_var = jnp.mean(centered * centered, axis=1, keepdims=True)
    return (centered / jnp.sqrt(row_var + 1e-05) * gain).astype(jnp.bfloat16)


def visit(depth, z, s, choose):
    j = s // 4
    low = z < depth - 1 - z
    near = choose(low, z, depth - 1 - z)
    far_way = choose(low, 1, -1)
    both = j <= 2 * near
    distance = choose(both, (j + 1) // 2, j - near)
    way = choose(both & (j % 2 == 1), -far_way, far_way)
    return z + way * distance


def arrivals(depth, program):
    chips = [(z, y, x) for z in range(depth) for y in range(2) for x in range(2)]
    events = [(0.0, k, chip, None) for k, chip in enumerate(chips)]
    count, free, seen, at = len(events), {}, {}, dict.fromkeys(chips, 0)

    def forward(chip, cls, origin, now):
        nonlocal count
        order = ORDERS[cls]
        for axis, step in (("z", 1), ("z", -1), ("y", 0), ("x", 0)):
            k = "zyx".index(axis)
            if any(chip["zyx".index(a)] != origin["zyx".index(a)] for a in order[order.index(axis) + 1:]):
                continue
            if axis == "z":
                target = chip[0] + step
                if not 0 <= target < depth or (chip[0] - origin[0]) * step < 0:
                    continue
            elif chip[k] != origin[k]:
                continue
            else:
                target = 1 - chip[k]
            peer = chip[:k] + (target,) + chip[k + 1:]
            end = max(free.get((chip, peer), 0.0), now) + 1.0
            free[chip, peer] = end
            heapq.heappush(events, (end + 0.55, count, peer, (cls, origin)))
            count += 1

    while events:
        now, _, chip, item = heapq.heappop(events)
        if item is not None:
            seen[(chip,) + item] = now
        if program is None:
            for cls, origin in [item] if item else [(c, chip) for c in range(len(ORDERS))]:
                forward(chip, cls, origin, now)
            continue
        while at[chip] < len(program):
            cls, s = program[at[chip]]
            z, y, x = chip
            origin = (visit(depth, z, s, lambda c, a, b: a if c else b), (y + s // 2) % 2, (x + s) % 2)
            if s > 0 and (chip, cls, origin) not in seen:
                break
            forward(chip, cls, origin, now)
            at[chip] += 1
    return chips, seen


def make_program(depth):
    program = None
    for _ in range(2):
        chips, seen = arrivals(depth, program)
        total = {}
        for z, y, x in chips:
            for cls in range(len(ORDERS)):
                for s in range(1, 4 * depth):
                    origin = (visit(depth, z, s, lambda c, a, b: a if c else b), (y + s // 2) % 2, (x + s) % 2)
                    total[cls, s] = total.get((cls, s), 0.0) + seen[(z, y, x), cls, origin]
        program = [(cls, 0) for cls in range(len(ORDERS))]
        program += sorted(total, key=lambda item: (round(total[item], 6), item))
    return program


def kernel(
    rows, program, fuse_norm, feat, weight_hbm, bias_hbm, gain_hbm, lookup_hbm, tiles, out,
    panel, held, acc, weight, bias, gain, lookup, send_sem, recv_sem, own_sem, tile_sem, small_sem,
):
    depth_z = rows // 8
    steps = depth_z * 4
    items = len(program)
    shard_rows, width = feat.shape
    piece_rows = shard_rows // len(ORDERS)
    row_blocks, slots, block = tiles.shape[0], tiles.shape[1], tiles.shape[2]
    shard_blocks = shard_rows // block
    piece_blocks = piece_rows // block

    me = lax.axis_index("rows")
    core = me % 2
    x = (me // 2) % 2
    y = (me // 4) % 2
    z = me // 8
    x_peer = me + 2 - 4 * x
    y_peer = me + 4 - 8 * y
    core_peer = me + 1 - 2 * core
    up, down = me + 8, me - 8
    has_up, has_down = z < depth_z - 1, z > 0

    own = pltpu.make_async_copy(feat, panel.at[me], own_sem)
    own.start()

    barrier = pltpu.get_barrier_semaphore()
    for peer in (x_peer, y_peer, core_peer):
        pl.semaphore_signal(barrier, inc=1, device_id={"rows": peer}, device_id_type=MESH)

    @pl.when(has_up)
    def _():
        pl.semaphore_signal(barrier, inc=1, device_id={"rows": up}, device_id_type=MESH)

    @pl.when(has_down)
    def _():
        pl.semaphore_signal(barrier, inc=1, device_id={"rows": down}, device_id_type=MESH)

    small_copies = [
        pltpu.make_async_copy(there, here, small_sem.at[k])
        for k, (there, here) in enumerate(
            ((lookup_hbm, lookup), (weight_hbm, weight), (bias_hbm, bias), (gain_hbm, gain))
        )
    ]
    tile_copies = [
        pltpu.make_async_copy(tiles.at[b], held.at[b, pl.ds(0, slots)], tile_sem.at[b])
        for b in range(row_blocks)
    ]
    for c in small_copies + tile_copies:
        c.start()
    own.wait()
    pl.semaphore_wait(barrier, 3 + jnp.where(has_up, 1, 0) + jnp.where(has_down, 1, 0))

    def chip_of(s):
        zs = visit(depth_z, z, s, jnp.where)
        return (zs * 2 + (y + s // 2) % 2) * 2 + (x + s) % 2, zs

    def copy(cls, origin, sem, peer):
        piece = panel.at[origin, pl.ds(cls * piece_rows, piece_rows)]
        return pltpu.make_async_remote_copy(
            src_ref=piece,
            dst_ref=piece,
            send_sem=send_sem.at[sem],
            recv_sem=recv_sem.at[cls, origin],
            device_id={"rows": peer},
            device_id_type=MESH,
        )

    numbers = {}

    def take(cls, s, act):
        chip, zs = chip_of(s)
        origin = chip * 2 + core
        order = ORDERS[cls]
        still = {"x": s % 2 == 0, "y": (s // 2) % 2 == 0, "z": s < 4}

        def send(name, peer, cond=None):
            sem = numbers.setdefault((cls, s, name), len(numbers))
            if cond is None:
                act(cls, origin, sem, peer)
            else:
                pl.when(cond)(functools.partial(act, cls, origin, sem, peer))

        def clear(axis):
            return all(still[a] for a in order[order.index(axis) + 1:])

        if clear("z"):
            if still["z"]:
                send("up", up, has_up)
                send("down", down, has_down)
            else:
                send("up", up, has_up & (zs < z))
                send("down", down, has_down & (zs > z))
        if clear("y") and still["y"]:
            send("y", y_peer)
        if clear("x") and still["x"]:
            send("x", x_peer)
        send("core", core_peer)

    def start(*what):
        copy(*what).start()

    def finish(*what):
        copy(*what).wait_send()

    def item_step(k):
        cls, s = program[k]
        if s > 0:
            copy(cls, chip_of(s)[0] * 2 + core, 0, core_peer).wait_recv()
        take(cls, s, start)

    def dispatch(i, low, high):
        if high - low == 1:
            item_step(low)
            return
        middle = (low + high) // 2
        pl.when(i < middle)(lambda: dispatch(i, low, middle))
        pl.when(i >= middle)(lambda: dispatch(i, middle, high))

    bits = (items - 1).bit_length()
    per_word = 30 // bits
    words = [
        sum((cls * steps + s) << (bits * k) for k, (cls, s) in enumerate(program[w:w + per_word]))
        for w in range(0, items, per_word)
    ]

    def entry(q):
        which = q // per_word
        word = jnp.int32(words[0])
        for k in range(1, len(words)):
            word = jnp.where(which == k, words[k], word)
        code = lax.shift_right_logical(word, (q - which * per_word) * bits) & (2**bits - 1)
        return code // steps, code % steps

    def multiply(q, carry):
        cls, s = entry(q)
        chip = chip_of(s)[0]
        copy(cls, chip * 2 + 1 - core, 0, core_peer).wait_recv()
        right = panel[pl.ds(chip * 2, 2), pl.ds(pl.multiple_of(cls * piece_rows, piece_rows), piece_rows)]
        right = right.reshape(2 * piece_rows, width)
        columns = [
            (chip * 2 + c) * shard_blocks + cls * piece_blocks + k
            for c in range(2) for k in range(piece_blocks)
        ]
        left = jnp.concatenate(
            [
                jnp.concatenate([held[b, lookup[b, c]] for c in columns], axis=1)
                for b in range(row_blocks)
            ],
            axis=0,
        )
        acc[...] += jnp.dot(left, right, preferred_element_type=jnp.float32)
        return carry

    acc[...] = jnp.zeros_like(acc)
    for b in range(row_blocks):
        held[b, slots] = jnp.zeros(held.shape[2:], held.dtype)

    begin = items // 8

    def done_after(i):
        return jnp.maximum(0, jnp.minimum(i, (i - begin) * 8 // 7))

    def step(i, carry):
        pl.when(i < items)(lambda: dispatch(i, 0, items))

        @pl.when(i == begin)
        def _():
            for c in small_copies + tile_copies:
                c.wait()

        lax.fori_loop(done_after(i - 1), done_after(i), multiply, 0)
        return carry

    lax.fori_loop(0, items + 1, step, 0)

    w = weight[...]
    for b in range(row_blocks):
        part = pl.ds(b * block, block)
        total = acc[part]
        high = total.astype(jnp.bfloat16)
        rest = (total - high.astype(jnp.float32)).astype(jnp.bfloat16)
        summed = jnp.dot(high, w, preferred_element_type=jnp.float32)
        summed += jnp.dot(rest, w, preferred_element_type=jnp.float32)
        if fuse_norm:
            out[part] = normed(jnp.maximum(summed + bias[...], 0.0), gain[...])
        else:
            out[part] = summed

    for cls, s in program:
        take(cls, s, finish)


def per_device(
    rows, reps, program, features, weight, shift_bias, norm_gain, tile_values, tile_cols, tile_counts, block_order
):
    row_blocks, _, slots, block, _ = tile_values.shape
    shard_rows, width = features.shape
    hidden_width = weight.shape[1]
    set_blocks = rows * shard_rows // block
    order = lax.dynamic_index_in_dim(block_order, lax.axis_index("rep"), 0, keepdims=False)
    numbers = jnp.arange(set_blocks, dtype=jnp.int32)
    number_at = jnp.sum(jnp.where(order[:, None] == numbers[None, :], numbers[:, None], 0), axis=0)
    ids = tile_cols.reshape(row_blocks, slots)
    slot = jnp.arange(slots, dtype=jnp.int32)[None, :]
    ids = jnp.where(slot < tile_counts.reshape(row_blocks, 1), ids, -1)
    hit = ids[:, :, None] == number_at[None, None, :]
    lookup = slots + jnp.sum(jnp.where(hit, slot[:, :, None] - slots, 0), axis=1)

    fuse_norm = reps == 1
    nodes = row_blocks * block
    vmem = pl.BlockSpec(memory_space=pltpu.VMEM)
    hbm = pl.BlockSpec(memory_space=pl.ANY)
    summed = pl.pallas_call(
        functools.partial(kernel, rows, program, fuse_norm),
        out_shape=jax.ShapeDtypeStruct(
            (nodes, hidden_width), jnp.bfloat16 if fuse_norm else jnp.float32
        ),
        in_specs=[hbm] * 6,
        out_specs=vmem,
        scratch_shapes=[
            pltpu.VMEM((rows, shard_rows, width), jnp.bfloat16),
            pltpu.VMEM((row_blocks, slots + 1, block, block), jnp.bfloat16),
            pltpu.VMEM((nodes, width), jnp.float32),
            pltpu.VMEM(weight.shape, weight.dtype),
            pltpu.VMEM((1, hidden_width), jnp.float32),
            pltpu.VMEM((1, hidden_width), jnp.float32),
            pltpu.SMEM(lookup.shape, jnp.int32),
            pltpu.SemaphoreType.DMA((5 * len(program),)),
            pltpu.SemaphoreType.DMA((len(ORDERS), rows)),
            pltpu.SemaphoreType.DMA,
            pltpu.SemaphoreType.DMA((row_blocks,)),
            pltpu.SemaphoreType.DMA((4,)),
        ],
        compiler_params=pltpu.CompilerParams(
            collective_id=0, has_side_effects=True, vmem_limit_bytes=60 * 1024 * 1024
        ),
    )(
        features, weight, shift_bias[None, :], norm_gain[None, :], lookup,
        tile_values.reshape(row_blocks, slots, block, block),
    )
    if fuse_norm:
        return summed
    mine = lax.psum_scatter(summed, "rep", scatter_dimension=0, tiled=True)
    return normed(jnp.maximum(mine + shift_bias, 0.0), norm_gain)


def solution(mesh):
    program = make_program(mesh.shape["rows"] // 8)
    in_specs = (
        P(("rows", "rep"), None),
        P(),
        P(),
        P(),
        P("rows", "rep", None, None, None),
        P("rows", "rep", None),
        P("rows", "rep"),
        P(),
    )
    out_specs = P(("rows", "rep"), None)
    return jax.shard_map(
        functools.partial(per_device, mesh.shape["rows"], mesh.shape["rep"], program),
        mesh=mesh, in_specs=in_specs, out_specs=out_specs, check_vma=False,
    )
```
